32 devices in a mesh: tm: 4 (over y, core), neuron: 4 (over z), motif: 2 (over x).
Axes of the slice: x: 2, y: 2, z: 4, core: 2. Of those that a mesh axis runs over, the one named last changes fastest.
Arguments:
- counts: int32 [1024, 4096], P('neuron', 'tm'), may hold values from 0 to 2
- motif_w: float32 [64, 64, 1024], P('motif', None, 'neuron'), may hold values from 0.05 to 3, as said below
- motif_h: float32 [64, 4096], P('motif', 'tm'), may hold values from 0.05 to 3, as said below
Outputs:
- new_w: float32 [64, 64, 1024], P('motif', None, 'neuron')
- new_h: float32 [64, 4096], P('motif', 'tm')
The draws below stay inside these ranges and needn't reach their ends.
Inputs may be any that keep to these rules, and one draw needn't show every extreme that they name: `motif_w`: positive factors. `motif_h`: positive activations.
All inputs are finite; a program needn't handle non-finite values.
Results may differ from the reference program's by a relative error of at most 0.0003.
Values may be sent and summed in bfloat16 or wider, within the bound.
A program may use at most 128 MiB of HBM per device.

```python
import jax
import jax.numpy as jnp
from jax import lax

MOTIFS = 64
LAGS = 64
NEUR_DEV = 256
BIN_DEV = 1024
ITERS = 2
NEURONS = 1024
TBINS = 4096


def strong_values(key, shape):
    base = jax.random.uniform(key, shape, jnp.float32)
    return 0.5 * jnp.exp(jnp.log(6.0) * base)


def draw_motif_w(key, part):
    values = strong_values(jax.random.fold_in(key, 11), (MOTIFS, LAGS, NEURONS))
    group = jnp.arange(MOTIFS, dtype=jnp.int32) // (MOTIFS // 2) % 2
    block = jnp.arange(NEURONS, dtype=jnp.int32) // NEUR_DEV % 2
    strong = group[:, None, None] == block[None, None, :]
    return jnp.where(strong, values, 0.1 * values).astype(jnp.float32)


def draw_motif_h(key, part):
    values = strong_values(jax.random.fold_in(key, 23), (MOTIFS, TBINS))
    group = jnp.arange(MOTIFS, dtype=jnp.int32) // (MOTIFS // 2) % 2
    block = jnp.arange(TBINS, dtype=jnp.int32) // BIN_DEV % 2
    strong = group[:, None] != block[None, :]
    return jnp.where(strong, values, 0.1 * values).astype(jnp.float32)


def place_ends(array, own_key, low, high):
    shape = array.shape
    index_at = [jax.random.randint(jax.random.fold_in(own_key, axis), (), 0, shape[axis]) for axis in range(len(shape))]
    array = array.at[tuple(index_at)].set(low)
    longest = shape.index(max(shape))
    index_at[longest] = (index_at[longest] + 1) % shape[longest]
    return array.at[tuple(index_at)].set(high)


def setup_inputs(seed: int = 0) -> dict:
    key_list = jax.random.split(jax.random.key(seed), 4)
    return {
        "counts": place_ends(jax.random.randint(key_list[0], (NEURONS, TBINS), 0, 3), jax.random.fold_in(key_list[0], 1), 0, 2).astype(jnp.int32),
        "motif_w": draw_motif_w(jax.random.fold_in(key_list[3], 71), 0),
        "motif_h": draw_motif_h(jax.random.fold_in(key_list[3], 71), 0),
    }


def stacked(hext, count, rim, width):
    rows = [hext[:, rim - lag: rim - lag + width] for lag in range(rim + 1)]
    return jnp.stack(rows, axis=1).reshape(count * (rim + 1), width)


def reference(counts, motif_w, motif_h):
    rim = LAGS - 1
    scale_factor = 1.0 / (MOTIFS * LAGS)
    weights = motif_w.reshape(MOTIFS * LAGS, NEURONS)
    acts = motif_h
    spike_events = counts.astype(jnp.float32)
    reduce_over_rows = (((0,), (0,)), ((), ()))
    contract_cols = (((1,), (1,)), ((), ()))

    def extend_padded(acts):
        zeros = jnp.zeros((MOTIFS, rim), jnp.bfloat16)
        return jnp.concatenate([zeros, acts.astype(jnp.bfloat16)], axis=1)

    def ratio_of(weight_bfloat, lagged_copies):
        estimated_counts = lax.dot_general(weight_bfloat, lagged_copies, reduce_over_rows, preferred_element_type=jnp.float32) * scale_factor
        return (spike_events / estimated_counts).astype(jnp.bfloat16)

    bins = jnp.arange(TBINS, dtype=jnp.int32)
    offsets = jnp.arange(LAGS, dtype=jnp.int32)
    mask = ((bins[None, :] + offsets[:, None]) < TBINS).astype(jnp.float32)
    for step in range(ITERS):
        weight_bfloat = weights.astype(jnp.bfloat16)
        lagged_copies = stacked(extend_padded(acts), MOTIFS, rim, TBINS)
        ratio = ratio_of(weight_bfloat, lagged_copies)
        rext = jnp.concatenate([ratio, jnp.zeros((NEURONS, rim), jnp.bfloat16)], axis=1)
        prod = jnp.dot(weight_bfloat, rext, preferred_element_type=jnp.float32).reshape(MOTIFS, LAGS, TBINS + rim)
        hnum = jnp.zeros((MOTIFS, TBINS), jnp.float32)
        for lag in range(LAGS):
            hnum = hnum + prod[:, lag, lag:lag + TBINS]
        colsum = jnp.sum(weight_bfloat.astype(jnp.float32).reshape(MOTIFS, LAGS, NEURONS), axis=2)
        hden = jnp.dot(colsum, mask, precision=lax.Precision.HIGHEST)
        acts = acts * hnum / hden
        lagged_copies = stacked(extend_padded(acts), MOTIFS, rim, TBINS)
        ratio = ratio_of(weight_bfloat, lagged_copies)
        wnum = lax.dot_general(lagged_copies, ratio, contract_cols, preferred_element_type=jnp.float32)
        wden = jnp.sum(lagged_copies, axis=1, dtype=jnp.float32)
        weights = weights * wnum / wden[:, None]
    return weights.reshape(MOTIFS, LAGS, NEURONS), acts
```

```python
import functools

import jax
import jax.numpy as jnp
from jax import lax
from jax.experimental import pallas as pl
from jax.experimental.pallas import tpu as pltpu
from jax.sharding import PartitionSpec as P

MOTIFS = 64
LAGS = 64
ITERS = 2
RIM = 128
MESH = pl.DeviceIdType.MESH
BF = jnp.bfloat16
F32 = jnp.float32


def remote(src, dst, send_sem, recv_sem, axis, peer):
    return pltpu.make_async_remote_copy(
        src_ref=src,
        dst_ref=dst,
        send_sem=send_sem,
        recv_sem=recv_sem,
        device_id={axis: peer},
        device_id_type=MESH,
    )


def kernel(
    sizes, counts_ref, w_ref, h_ref, w_out, h_out,
    hf, hs, wb, wbt, part, xsend, xrecv, rall, rext, rhalo, hpart, hsend, hrecv, hag, hall, h0send, h0recv,
    wsend, wrecv,
    x_ss, x_rs, h0_ss, h0_rs, rh_ss, rh_rs, hr_ss, hr_rs, ha_ss, ha_rs, ht_ss, ht_rs, ra_ss, ra_rs, w_ss, w_rs,
):
    tms, neurs, mots = sizes
    t, j, m = lax.axis_index("tm"), lax.axis_index("neuron"), lax.axis_index("motif")
    chips = tms // 2
    y, core = t // 2, t % 2
    buddy = 2 * y + 1 - core
    kl, n = w_ref.shape
    lags = LAGS
    k_dev = kl // lags
    kpn, width = h_ref.shape[1:]
    chunks, _, cw = part.shape
    blk = 4 * lags
    wide = width + RIM
    scale = 1.0 / (MOTIFS * LAGS)
    total_bins = width * tms

    barrier = pltpu.get_barrier_semaphore()
    for o in range(1, tms):
        pl.semaphore_signal(barrier, inc=1, device_id={"tm": lax.rem(t + o, tms)}, device_id_type=MESH)
    for o in range(1, neurs):
        pl.semaphore_signal(barrier, inc=1, device_id={"neuron": lax.rem(j + o, neurs)}, device_id_type=MESH)
    for o in range(1, mots):
        pl.semaphore_signal(barrier, inc=1, device_id={"motif": lax.rem(m + o, mots)}, device_id_type=MESH)
    pl.semaphore_wait(barrier, tms + neurs + mots - 3)

    sub = lax.broadcasted_iota(jnp.int32, (8, wide), 0)

    def toeplitz(block, halo, index, slot):
        hf[:, :RIM] = jnp.where(index > 0, halo.astype(F32), 0.0)
        hf[:, RIM:] = block.astype(F32)

        def one(k, _):
            base = jnp.broadcast_to(hf[pl.ds(k, 1), :], (8, wide))
            for bit in (1, 2, 4):
                base = jnp.where((sub & bit) != 0, pltpu.roll(base, bit, 1), base)
            rows = [base[:, RIM:]]
            for i in range(1, lags // 8):
                rows.append(pltpu.roll(base, 8 * i, 1)[:, RIM:])
            at = pl.multiple_of(k * lags, lags)
            hs[slot, pl.ds(at, lags), :] = jnp.concatenate(rows, axis=0).astype(BF)
            return 0

        lax.fori_loop(0, k_dev, one, 0)

    def xcopy(phase, o, c):
        return remote(
            xsend.at[c], xrecv.at[phase, o - 1, c], x_ss.at[o - 1, c], x_rs.at[phase, o - 1, c],
            "motif", lax.rem(m + o, mots),
        )

    def xhat_send(phase):
        def one(c, _):
            cols = pl.ds(pl.multiple_of(c * cw, cw), cw)
            acc = jnp.dot(wbt[...], hs[y, :, cols], preferred_element_type=F32) * scale
            part[c] = acc
            xsend[c] = acc.astype(BF)
            for o in range(1, mots):
                xcopy(phase, o, c).start()
            return 0

        lax.fori_loop(0, chunks, one, 0)

    def ratio(phase, c):
        total = part[c]
        for o in range(1, mots):
            xcopy(phase, o, c).wait()
            total = total + xrecv[phase, o - 1, c].astype(F32)
        cols = pl.ds(pl.multiple_of(c * cw, cw), cw)
        return (counts_ref[:, cols].astype(F32) / total).astype(BF)

    for jj in range(neurs):
        hpart[jj * kpn : (jj + 1) * kpn, :width] = h_ref[jj]
    h0send[...] = hpart[:, width - RIM : width].astype(BF)
    h0 = remote(h0send, h0recv, h0_ss.at[0], h0_rs.at[0], "tm", lax.rem(t + 1, tms))
    h0.start()

    def first_weights(q, _):
        rows = pl.ds(pl.multiple_of(q * blk, blk), blk)
        value = w_ref[rows, :]
        wb[rows, :] = value.astype(BF)
        wbt[:, rows] = value.T.astype(BF)
        return 0

    lax.fori_loop(0, kl // blk, first_weights, 0)
    h0.wait()
    toeplitz(hpart[:, :width].astype(BF), h0recv[...], t, y)

    for it in range(ITERS):
        phase = 2 * it
        xhat_send(phase)

        def first_ratio(c, _):
            cols = pl.ds(pl.multiple_of(c * cw, cw), cw)
            rext[:, cols] = ratio(phase, c)
            return 0

        first_ratio(0, 0)
        halo = remote(
            rext.at[:, 0:RIM], rhalo.at[it], rh_ss.at[it], rh_rs.at[it], "tm", lax.rem(t + tms - 1, tms)
        )
        halo.start()
        lax.fori_loop(1, chunks, first_ratio, 0)
        halo.wait()
        lane = lax.broadcasted_iota(jnp.int32, (n, RIM), 1)
        after = jnp.where(t < tms - 1, rhalo[it].astype(F32), 0.0)
        rext[:, width:] = jnp.where(lane == RIM - 1, 1.0, after).astype(BF)

        lag_at = lax.broadcasted_iota(jnp.int32, (lags, RIM), 0)
        bin_at = lax.broadcasted_iota(jnp.int32, (lags, RIM), 1) + (t * width + width - RIM)
        inside = lag_at + bin_at < total_bins

        def numerators(q, _):
            rows = pl.ds(pl.multiple_of(q * blk, blk), blk)
            prod = jnp.dot(wb[rows, :], rext[...], preferred_element_type=F32)
            for kk in range(blk // lags):
                one = prod[kk * lags : (kk + 1) * lags, :]
                acc = one[0:8, :]
                for i in range(1, lags // 8):
                    acc = acc + pltpu.roll(one[8 * i : 8 * i + 8, :], wide - 8 * i, 1)
                for bit in (1, 2, 4):
                    acc = jnp.where((sub & bit) != 0, pltpu.roll(acc, wide - bit, 1), acc)
                num = jnp.sum(acc, axis=0, keepdims=True)
                colsum = one[:, wide - 1 : wide]
                den = jnp.sum(jnp.where(inside, colsum, 0.0), axis=0, keepdims=True)
                k = q * (blk // lags) + kk
                hpart[pl.ds(k, 1), :] = jnp.concatenate([num[:, :width], den], axis=1)
            return 0

        lax.fori_loop(0, kl // blk, numerators, 0)

        for jj in range(neurs):
            hsend[jj] = hpart[jj * kpn : (jj + 1) * kpn, :]
        copies = []
        for o in range(1, neurs):
            peer = lax.rem(j + o, neurs)
            copies.append(remote(
                hsend.at[peer], hrecv.at[it, o - 1], hr_ss.at[it, o - 1], hr_rs.at[it, o - 1], "neuron", peer
            ))
            copies[-1].start()
        total = hsend[j]
        for o in range(1, neurs):
            copies[o - 1].wait()
            total = total + hrecv[it, o - 1]
        den = jnp.concatenate(
            [jnp.broadcast_to(total[:, width : width + 1], (kpn, width - RIM)), total[:, width:]], axis=1
        )
        old = h_ref[j] if it == 0 else hag[it - 1, j]
        hag[it, j] = old * total[:, :width] / den
        copies = []
        for o in range(1, neurs):
            copies.append(remote(
                hag.at[it, j], hag.at[it, j], ha_ss.at[it, o - 1], ha_rs.at[it, o - 1],
                "neuron", lax.rem(j + o, neurs),
            ))
            copies[-1].start()
        for copy in copies:
            copy.wait()
        for jj in range(neurs):
            hpart[jj * kpn : (jj + 1) * kpn, :width] = hag[it, jj]
        hall[it, t] = hpart[:, :width].astype(BF)
        copies = []
        for o in range(1, tms):
            copies.append(remote(
                hall.at[it, t], hall.at[it, t], ht_ss.at[it, o - 1], ht_rs.at[it, o - 1],
                "tm", lax.rem(t + o, tms),
            ))
            copies[-1].start()
        copies[0].wait()
        back = lax.rem(t + tms - 1, tms)
        toeplitz(hall[it, t], hall[it, back, :, width - RIM :], t, y)

        phase = 2 * it + 1
        xhat_send(phase)
        for copy in copies[1:]:
            copy.wait()

        def rcopy(d, c):
            return remote(
                rall.at[it, y, c], rall.at[it, y, c], ra_ss.at[it, d - 1, c], ra_rs.at[it, d - 1, c],
                "tm", 2 * lax.rem(y + d, chips) + core,
            )

        def second_ratio(c, _):
            rall[it, y, c] = ratio(phase, c)
            for d in range(1, chips):
                rcopy(d, c).start()
            return 0

        lax.fori_loop(0, chunks, second_ratio, 0)
        for d in range(1, chips):
            slot = lax.rem(y + d, chips)
            index = 2 * slot + core
            toeplitz(hall[it, index], hall[it, lax.rem(index + tms - 1, tms), :, width - RIM :], index, slot)
        lag_at = lax.broadcasted_iota(jnp.int32, (lags, width), 0)
        bin_at = lax.broadcasted_iota(jnp.int32, (lags, width), 1)
        wden = jnp.zeros((lags, k_dev), F32)
        for i in range(tms):
            mask = jnp.where(lag_at + bin_at + i * width < total_bins, 1.0, 0.0).astype(BF)
            wden = wden + lax.dot_general(
                mask, hall[it, i], (((1,), (1,)), ((), ())), preferred_element_type=F32
            )

        def wait_ratio(c, _):
            for d in range(1, chips):
                rcopy(d, c).wait()
            return 0

        lax.fori_loop(0, chunks, wait_ratio, 0)

        def wcopy(q):
            rows = pl.ds(pl.multiple_of(q * blk, blk), blk)
            return remote(
                wsend.at[rows, :], wrecv.at[it, rows, :], w_ss.at[it, q], w_rs.at[it, q], "tm", buddy
            )

        def factor(q, _):
            rows = pl.ds(pl.multiple_of(q * blk, blk), blk)
            acc = jnp.zeros((blk, n), F32)
            for yy in range(chips):
                for c in range(chunks):
                    acc = acc + lax.dot_general(
                        hs[yy, rows, c * cw : (c + 1) * cw], rall[it, yy, c],
                        (((1,), (1,)), ((), ())), preferred_element_type=F32,
                    )
            wsend[rows, :] = acc
            wcopy(q).start()
            return 0

        lax.fori_loop(0, kl // blk, factor, 0)
        for q in range(kl // blk):
            wcopy(q).wait()
            for kk in range(blk // lags):
                k = q * (blk // lags) + kk
                rows = slice(k * lags, (k + 1) * lags)
                old = w_ref[rows, :] if it == 0 else w_out[rows, :]
                new = old * (wsend[rows, :] + wrecv[it, rows, :]) / wden[:, k : k + 1]
                w_out[rows, :] = new
            if it < ITERS - 1:
                rows = slice(q * blk, (q + 1) * blk)
                value = w_out[rows, :]
                wb[rows, :] = value.astype(BF)
                wbt[:, rows] = value.T.astype(BF)
    h_out[...] = hag[ITERS - 1]


def local(sizes, counts, motif_w, motif_h):
    tms, neurs, mots = sizes
    k_dev, lags, n = motif_w.shape
    width = counts.shape[1]
    kl = k_dev * lags
    kpn = k_dev // neurs
    cw = 256
    chunks = width // cw
    chips = tms // 2
    wide = width + RIM
    blocks = kl // (4 * lags)
    vmem = pltpu.VMEM
    dma = pltpu.SemaphoreType.DMA
    o_t, o_n, o_m, o_y = tms - 1, max(neurs - 1, 1), max(mots - 1, 1), max(chips - 1, 1)
    new_w, new_h = pl.pallas_call(
        functools.partial(kernel, sizes),
        out_shape=(
            jax.ShapeDtypeStruct((kl, n), F32),
            jax.ShapeDtypeStruct((neurs, kpn, width), F32),
        ),
        in_specs=[pl.BlockSpec(memory_space=vmem)] * 3,
        out_specs=[pl.BlockSpec(memory_space=vmem)] * 2,
        scratch_shapes=[
            vmem((k_dev, wide), F32),
            vmem((chips, kl, width), BF),
            vmem((kl, n), BF),
            vmem((n, kl), BF),
            vmem((chunks, n, cw), F32),
            vmem((chunks, n, cw), BF),
            vmem((2 * ITERS, o_m, chunks, n, cw), BF),
            vmem((ITERS, chips, chunks, n, cw), BF),
            vmem((n, wide), BF),
            vmem((ITERS, n, RIM), BF),
            vmem((k_dev, wide), F32),
            vmem((neurs, kpn, wide), F32),
            vmem((ITERS, o_n, kpn, wide), F32),
            vmem((ITERS, neurs, kpn, width), F32),
            vmem((ITERS, tms, k_dev, width), BF),
            vmem((k_dev, RIM), BF),
            vmem((k_dev, RIM), BF),
            vmem((kl, n), F32),
            vmem((ITERS, kl, n), F32),
            dma((o_m, chunks)),
            dma((2 * ITERS, o_m, chunks)),
            dma((1,)),
            dma((1,)),
            dma((ITERS,)),
            dma((ITERS,)),
            dma((ITERS, o_n)),
            dma((ITERS, o_n)),
            dma((ITERS, o_n)),
            dma((ITERS, o_n)),
            dma((ITERS, o_t)),
            dma((ITERS, o_t)),
            dma((ITERS, o_y, chunks)),
            dma((ITERS, o_y, chunks)),
            dma((ITERS, blocks)),
            dma((ITERS, blocks)),
        ],
        compiler_params=pltpu.CompilerParams(
            collective_id=0, has_side_effects=True, vmem_limit_bytes=56 * 2**20
        ),
    )(counts, motif_w.reshape(kl, n), motif_h.reshape(neurs, kpn, width))
    return new_w.reshape(k_dev, lags, n), new_h.reshape(k_dev, width)


def solution(mesh):
    sizes = (mesh.shape["tm"], mesh.shape["neuron"], mesh.shape["motif"])
    in_specs = (P("neuron", "tm"), P("motif", None, "neuron"), P("motif", "tm"))
    out_specs = (P("motif", None, "neuron"), P("motif", "tm"))
    return jax.shard_map(
        functools.partial(local, sizes), mesh=mesh, in_specs=in_specs, out_specs=out_specs, check_vma=False
    )
```

```python
import functools

import jax
import jax.numpy as jnp
from jax import lax
from jax.experimental import pallas as pl
from jax.experimental.pallas import tpu as pltpu
from jax.sharding import PartitionSpec as P

MOTIFS = 64
LAGS = 64
ITERS = 2
RIM = 128
MESH = pl.DeviceIdType.MESH
BF = jnp.bfloat16
F32 = jnp.float32


def remote(src, dst, send_sem, recv_sem, axis, peer):
    return pltpu.make_async_remote_copy(
        src_ref=src,
        dst_ref=dst,
        send_sem=send_sem,
        recv_sem=recv_sem,
        device_id={axis: peer},
        device_id_type=MESH,
    )


def kernel(
    sizes, counts_ref, w_ref, h_ref, w_out, h_out,
    hf, hs, wb, wbt, part, xsend, xrecv, rall, rext, rhalo, hpart, hsend, hrecv, hag, hall, h0send, h0recv,
    wsend, wrecv,
    x_ss, x_rs, h0_ss, h0_rs, rh_ss, rh_rs, hr_ss, hr_rs, ha_ss, ha_rs, ht_ss, ht_rs, ra_ss, ra_rs, w_ss, w_rs,
):
    tms, neurs, mots = sizes
    t, j, m = lax.axis_index("tm"), lax.axis_index("neuron"), lax.axis_index("motif")
    chips = tms // 2
    y, core = t // 2, t % 2
    buddy = 2 * y + 1 - core
    kl, n = w_ref.shape
    lags = LAGS
    k_dev = kl // lags
    kpn, width = h_ref.shape[1:]
    chunks, _, cw = part.shape
    blk = 4 * lags
    wide = width + RIM
    scale = 1.0 / (MOTIFS * LAGS)
    total_bins = width * tms

    barrier = pltpu.get_barrier_semaphore()
    for o in range(1, tms):
        pl.semaphore_signal(barrier, inc=1, device_id={"tm": lax.rem(t + o, tms)}, device_id_type=MESH)
    for o in range(1, neurs):
        pl.semaphore_signal(barrier, inc=1, device_id={"neuron": lax.rem(j + o, neurs)}, device_id_type=MESH)
    for o in range(1, mots):
        pl.semaphore_signal(barrier, inc=1, device_id={"motif": lax.rem(m + o, mots)}, device_id_type=MESH)
    pl.semaphore_wait(barrier, tms + neurs + mots - 3)

    sub = lax.broadcasted_iota(jnp.int32, (8, wide), 0)

    def toeplitz(block, halo, index, slot):
        hf[:, :RIM] = jnp.where(index > 0, halo.astype(F32), 0.0)
        hf[:, RIM:] = block.astype(F32)

        def one(k, _):
            base = jnp.broadcast_to(hf[pl.ds(k, 1), :], (8, wide))
            base = pltpu.roll(base, 0, 1, stride=1, stride_axis=0)
            base = jnp.concatenate([base, pltpu.roll(base, 8, 1)], axis=0).astype(BF)
            for i in range(lags // 16):
                at = pl.multiple_of(k * lags + 16 * i, 16)
                hs[slot, pl.ds(at, 16), :] = base[:, RIM - 16 * i : RIM - 16 * i + width]
            return 0

        lax.fori_loop(0, k_dev, one, 0, unroll=4)

    def xcopy(phase, o, c):
        return remote(
            xsend.at[c], xrecv.at[phase, o - 1, c], x_ss.at[o - 1, c], x_rs.at[phase, o - 1, c],
            "motif", lax.rem(m + o, mots),
        )

    def xhat_send(phase):
        def one(c, _):
            cols = pl.ds(pl.multiple_of(c * cw, cw), cw)
            acc = jnp.dot(wbt[...], hs[y, :, cols], preferred_element_type=F32) * scale
            part[c] = acc
            xsend[c] = acc.astype(BF)
            for o in range(1, mots):
                xcopy(phase, o, c).start()
            return 0

        lax.fori_loop(0, chunks, one, 0)

    def ratio(phase, c):
        total = part[c]
        for o in range(1, mots):
            xcopy(phase, o, c).wait()
            total = total + xrecv[phase, o - 1, c].astype(F32)
        cols = pl.ds(pl.multiple_of(c * cw, cw), cw)
        return (counts_ref[:, cols].astype(F32) / total).astype(BF)

    for jj in range(neurs):
        hpart[jj * kpn : (jj + 1) * kpn, :width] = h_ref[jj]
    h0send[...] = hpart[:, width - RIM : width].astype(BF)
    h0 = remote(h0send, h0recv, h0_ss.at[0], h0_rs.at[0], "tm", lax.rem(t + 1, tms))
    h0.start()

    def first_weights(q, _):
        rows = pl.ds(pl.multiple_of(q * blk, blk), blk)
        value = w_ref[rows, :]
        wb[rows, :] = value.astype(BF)
        wbt[:, rows] = value.T.astype(BF)
        return 0

    lax.fori_loop(0, kl // blk, first_weights, 0)
    h0.wait()
    toeplitz(hpart[:, :width].astype(BF), h0recv[...], t, y)

    for it in range(ITERS):
        phase = 2 * it
        xhat_send(phase)

        def first_ratio(c, _):
            cols = pl.ds(pl.multiple_of(c * cw, cw), cw)
            rext[:, cols] = ratio(phase, c)
            return 0

        first_ratio(0, 0)
        halo = remote(
            rext.at[:, 0:RIM], rhalo.at[it], rh_ss.at[it], rh_rs.at[it], "tm", lax.rem(t + tms - 1, tms)
        )
        halo.start()
        lax.fori_loop(1, chunks, first_ratio, 0)
        halo.wait()
        lane = lax.broadcasted_iota(jnp.int32, (n, RIM), 1)
        after = jnp.where(t < tms - 1, rhalo[it].astype(F32), 0.0)
        rext[:, width:] = jnp.where(lane == RIM - 1, 1.0, after).astype(BF)

        lag_at = lax.broadcasted_iota(jnp.int32, (lags, RIM), 0)
        bin_at = lax.broadcasted_iota(jnp.int32, (lags, RIM), 1) + (t * width + width - RIM)
        inside = lag_at + bin_at < total_bins

        def numerators(q, _):
            rows = pl.ds(pl.multiple_of(q * blk, blk), blk)
            prod = jnp.dot(wb[rows, :], rext[...], preferred_element_type=F32)
            for kk in range(blk // lags):
                one = prod[kk * lags : (kk + 1) * lags, :]
                acc = one[0:8, :]
                for i in range(1, lags // 8):
                    acc = acc + pltpu.roll(one[8 * i : 8 * i + 8, :], wide - 8 * i, 1)
                for bit in (1, 2, 4):
                    acc = jnp.where((sub & bit) != 0, pltpu.roll(acc, wide - bit, 1), acc)
                num = jnp.sum(acc, axis=0, keepdims=True)
                colsum = one[:, wide - 1 : wide]
                den = jnp.sum(jnp.where(inside, colsum, 0.0), axis=0, keepdims=True)
                k = q * (blk // lags) + kk
                hpart[pl.ds(k, 1), :] = jnp.concatenate([num[:, :width], den], axis=1)
            return 0

        lax.fori_loop(0, kl // blk, numerators, 0)

        for jj in range(neurs):
            hsend[jj] = hpart[jj * kpn : (jj + 1) * kpn, :]
        copies = []
        for o in range(1, neurs):
            peer = lax.rem(j + o, neurs)
            copies.append(remote(
                hsend.at[peer], hrecv.at[it, o - 1], hr_ss.at[it, o - 1], hr_rs.at[it, o - 1], "neuron", peer
            ))
            copies[-1].start()
        total = hsend[j]
        for o in range(1, neurs):
            copies[o - 1].wait()
            total = total + hrecv[it, o - 1]
        den = jnp.concatenate(
            [jnp.broadcast_to(total[:, width : width + 1], (kpn, width - RIM)), total[:, width:]], axis=1
        )
        old = h_ref[j] if it == 0 else hag[it - 1, j]
        hag[it, j] = old * total[:, :width] / den
        copies = []
        for o in range(1, neurs):
            copies.append(remote(
                hag.at[it, j], hag.at[it, j], ha_ss.at[it, o - 1], ha_rs.at[it, o - 1],
                "neuron", lax.rem(j + o, neurs),
            ))
            copies[-1].start()
        for copy in copies:
            copy.wait()
        for jj in range(neurs):
            hpart[jj * kpn : (jj + 1) * kpn, :width] = hag[it, jj]
        hall[it, t] = hpart[:, :width].astype(BF)
        copies = []
        for o in range(1, tms):
            copies.append(remote(
                hall.at[it, t], hall.at[it, t], ht_ss.at[it, o - 1], ht_rs.at[it, o - 1],
                "tm", lax.rem(t + o, tms),
            ))
            copies[-1].start()
        copies[0].wait()
        back = lax.rem(t + tms - 1, tms)
        toeplitz(hall[it, t], hall[it, back, :, width - RIM :], t, y)

        phase = 2 * it + 1
        xhat_send(phase)
        for copy in copies[1:]:
            copy.wait()

        for d in range(1, chips):
            slot = lax.rem(y + d, chips)
            index = 2 * slot + core
            toeplitz(hall[it, index], hall[it, lax.rem(index + tms - 1, tms), :, width - RIM :], index, slot)
        lag_at = lax.broadcasted_iota(jnp.int32, (lags, width), 0)
        bin_at = lax.broadcasted_iota(jnp.int32, (lags, width), 1)
        wden = jnp.zeros((lags, k_dev), F32)
        for i in range(tms):
            mask = jnp.where(lag_at + bin_at + i * width < total_bins, 1.0, 0.0).astype(BF)
            wden = wden + lax.dot_general(
                mask, hall[it, i], (((1,), (1,)), ((), ())), preferred_element_type=F32
            )

        def rcopy(d, c):
            return remote(
                rall.at[it, y, c], rall.at[it, y, c], ra_ss.at[it, d - 1, c], ra_rs.at[it, d - 1, c],
                "tm", 2 * lax.rem(y + d, chips) + core,
            )

        def second_ratio(c, _):
            rall[it, y, c] = ratio(phase, c)
            for d in range(1, chips):
                rcopy(d, c).start()
            return 0

        lax.fori_loop(0, chunks, second_ratio, 0)
        def wait_ratio(c, _):
            for d in range(1, chips):
                rcopy(d, c).wait()
            return 0

        lax.fori_loop(0, chunks, wait_ratio, 0)

        def wcopy(q):
            rows = pl.ds(pl.multiple_of(q * blk, blk), blk)
            return remote(
                wsend.at[rows, :], wrecv.at[it, rows, :], w_ss.at[it, q], w_rs.at[it, q], "tm", buddy
            )

        def factor(q, _):
            rows = pl.ds(pl.multiple_of(q * blk, blk), blk)
            acc = jnp.zeros((blk, n), F32)
            for yy in range(chips):
                for c in range(chunks):
                    acc = acc + lax.dot_general(
                        hs[yy, rows, c * cw : (c + 1) * cw], rall[it, yy, c],
                        (((1,), (1,)), ((), ())), preferred_element_type=F32,
                    )
            wsend[rows, :] = acc
            wcopy(q).start()
            return 0

        lax.fori_loop(0, kl // blk, factor, 0)
        for q in range(kl // blk):
            wcopy(q).wait()
            for kk in range(blk // lags):
                k = q * (blk // lags) + kk
                rows = slice(k * lags, (k + 1) * lags)
                old = w_ref[rows, :] if it == 0 else w_out[rows, :]
                new = old * (wsend[rows, :] + wrecv[it, rows, :]) / wden[:, k : k + 1]
                w_out[rows, :] = new
            if it < ITERS - 1:
                rows = slice(q * blk, (q + 1) * blk)
                value = w_out[rows, :]
                wb[rows, :] = value.astype(BF)
                wbt[:, rows] = value.T.astype(BF)
    h_out[...] = hag[ITERS - 1]


def local(sizes, counts, motif_w, motif_h):
    tms, neurs, mots = sizes
    k_dev, lags, n = motif_w.shape
    width = counts.shape[1]
    kl = k_dev * lags
    kpn = k_dev // neurs
    cw = 256
    chunks = width // cw
    chips = tms // 2
    wide = width + RIM
    blocks = kl // (4 * lags)
    vmem = pltpu.VMEM
    dma = pltpu.SemaphoreType.DMA
    o_t, o_n, o_m, o_y = tms - 1, max(neurs - 1, 1), max(mots - 1, 1), max(chips - 1, 1)
    new_w, new_h = pl.pallas_call(
        functools.partial(kernel, sizes),
        out_shape=(
            jax.ShapeDtypeStruct((kl, n), F32),
            jax.ShapeDtypeStruct((neurs, kpn, width), F32),
        ),
        in_specs=[pl.BlockSpec(memory_space=vmem)] * 3,
        out_specs=[pl.BlockSpec(memory_space=vmem)] * 2,
        scratch_shapes=[
            vmem((k_dev, wide), F32),
            vmem((chips, kl, width), BF),
            vmem((kl, n), BF),
            vmem((n, kl), BF),
            vmem((chunks, n, cw), F32),
            vmem((chunks, n, cw), BF),
            vmem((2 * ITERS, o_m, chunks, n, cw), BF),
            vmem((ITERS, chips, chunks, n, cw), BF),
            vmem((n, wide), BF),
            vmem((ITERS, n, RIM), BF),
            vmem((k_dev, wide), F32),
            vmem((neurs, kpn, wide), F32),
            vmem((ITERS, o_n, kpn, wide), F32),
            vmem((ITERS, neurs, kpn, width), F32),
            vmem((ITERS, tms, k_dev, width), BF),
            vmem((k_dev, RIM), BF),
            vmem((k_dev, RIM), BF),
            vmem((kl, n), F32),
            vmem((ITERS, kl, n), F32),
            dma((o_m, chunks)),
            dma((2 * ITERS, o_m, chunks)),
            dma((1,)),
            dma((1,)),
            dma((ITERS,)),
            dma((ITERS,)),
            dma((ITERS, o_n)),
            dma((ITERS, o_n)),
            dma((ITERS, o_n)),
            dma((ITERS, o_n)),
            dma((ITERS, o_t)),
            dma((ITERS, o_t)),
            dma((ITERS, o_y, chunks)),
            dma((ITERS, o_y, chunks)),
            dma((ITERS, blocks)),
            dma((ITERS, blocks)),
        ],
        compiler_params=pltpu.CompilerParams(
            collective_id=0, has_side_effects=True, vmem_limit_bytes=56 * 2**20
        ),
    )(counts, motif_w.reshape(kl, n), motif_h.reshape(neurs, kpn, width))
    return new_w.reshape(k_dev, lags, n), new_h.reshape(k_dev, width)


def solution(mesh):
    sizes = (mesh.shape["tm"], mesh.shape["neuron"], mesh.shape["motif"])
    in_specs = (P("neuron", "tm"), P("motif", None, "neuron"), P("motif", "tm"))
    out_specs = (P("motif", None, "neuron"), P("motif", "tm"))
    return jax.shard_map(
        functools.partial(local, sizes), mesh=mesh, in_specs=in_specs, out_specs=out_specs, check_vma=False
    )
```
